512 devices in a mesh: mom: 128 (over x, z_hi, y), row: 2 (over core), col: 2 (over z_lo).
Axes of the slice: x: 4, y: 8, z: 8 (z_hi: 4, z_lo: 2; z = z_hi * 2 + z_lo), core: 2. Of those that a mesh axis runs over, the one named last changes fastest.
Arguments:
- left_part: bfloat16 [128, 1536, 1536], P('mom', 'row', 'col'), may hold values from -0.15625 to 0.15625
- vertex: bfloat16 [128, 1536, 1536], P('mom', 'row', 'col'), may hold values from -6 to 6
- bubble: float32 [128, 1536], P('mom'), may hold values from 0.25 to 2
- cross_map: int32 [1536, 128], P(('col', 'mom')), may hold values from 0 to 127, each once within a row
Outputs:
- crossed: bfloat16 [1536, 128, 1536], P(('col', 'mom'), None, 'row')
The draws below stay inside these ranges and needn't reach their ends.
Inputs may be any that keep to these rules, and one draw needn't show every extreme that they name: Each row cross_map[b, :] is a permutation of the 128 transfer momenta.
All inputs are finite; a program needn't handle non-finite values.
Results may differ from the reference program's by a relative error of at most 0.0055.
Values may be sent and summed in bfloat16 or wider, within the bound.
A program may use at most 64 MiB of HBM per device.

```python
import jax
import jax.numpy as jnp
from jax import lax

M = 1536
NQ = 128


def block_levels(rng, extent, cuts, smallest, top_value):
    def one(position, parts):
        draws = jax.random.uniform(jax.random.fold_in(jax.random.fold_in(rng, 6), position), (parts,), jnp.float32, smallest / len(cuts), top_value / len(cuts))
        return jnp.repeat(jnp.exp(draws), extent[position] // parts).reshape((-1,) + (1,) * (len(extent) - position - 1))

    loudness = one(*cuts[0])
    for cut in cuts[1:]:
        loudness = loudness * one(*cut)
    return loudness


def gaussian(own_key, extent, scale, most, shards=(), kind=jnp.bfloat16):
    values = scale * jax.random.normal(own_key, extent, jnp.float32)
    if shards:
        values = values * block_levels(own_key, extent, shards, -0.22, 0.18)
    return jnp.clip(values, -most, most).astype(kind)


def setup_inputs(seed: int = 0) -> dict:
    key_of = jax.random.split(jax.random.key(seed), 5)
    return {
        "left_part": gaussian(key_of[0], (NQ, M, M), M ** -0.5, 0.15625, ((0, 128), (1, 2), (2, 2))),
        "vertex": gaussian(key_of[1], (NQ, M, M), 1.0, 6.0, ((0, 128), (1, 2), (2, 2))),
        "bubble": jnp.clip(0.25 + 1.75 * jax.random.uniform(key_of[2], (NQ, M), jnp.float32) ** block_levels(key_of[2], (NQ, M), ((0, 128),), -0.2, 0.2), 0.25, 2.0),
        "cross_map": jax.vmap(lambda own: jax.random.permutation(own, NQ))(jax.random.split(key_of[3], M)).reshape((M, NQ)).astype(jnp.int32),
    }


def one_momentum(operands):
    left_part, vertex, bubble = operands
    weighted = (left_part.astype(jnp.float32) * bubble[None, :]).astype(jnp.bfloat16)
    first = jnp.dot(weighted, vertex, preferred_element_type=jnp.float32)
    first_round = first.astype(jnp.bfloat16)
    second = jnp.dot(weighted, first_round, preferred_element_type=jnp.float32)
    return (vertex.astype(jnp.float32) + first + second).astype(jnp.bfloat16)


def reference(left_part, vertex, bubble, cross_map):
    corrected = lax.map(one_momentum, (left_part, vertex, bubble))

    def cross_column(operands):
        column, mapping = operands
        return corrected[mapping, :, column]

    columns = jnp.arange(M, dtype=jnp.int32)
    return lax.map(cross_column, (columns, cross_map.astype(jnp.int32)))
```

```python
import functools

import jax
import jax.numpy as jnp
from jax import lax
from jax.experimental import pallas as pl
from jax.experimental.pallas import tpu as pltpu
from jax.sharding import PartitionSpec as P

MESH = pl.DeviceIdType.MESH
F32 = jnp.float32
BF16 = jnp.bfloat16
LANES = 128


def nt(lhs, rhs):
    return lax.dot_general(lhs, rhs, (((1,), (1,)), ((), ())), preferred_element_type=F32)


def kernel(
    momenta, left_ref, vertex_ref, bubble_ref, map_ref, out_ref,
    left_own, left_got, vertex_own, vertex_got, weighted, flipped, first, first_round,
    choose, sent, got, result,
    local_sem, left_send, left_recv, vertex_send, vertex_recv, first_send, first_recv,
    move_send, move_recv, keep_sem, out_sem,
):
    half = left_own.shape[0]
    per_device = half // momenta
    parts, _, span = result.shape
    blocks = span // LANES
    chunks = left_send.shape[0]
    rows = half // chunks
    me = lax.axis_index("mom")
    row = lax.axis_index("row")
    col = lax.axis_index("col")
    across = {"col": 1 - col}
    beside = {"row": 1 - row}

    barrier = pltpu.get_barrier_semaphore()
    pl.semaphore_signal(barrier, inc=1, device_id=across, device_id_type=MESH)
    pl.semaphore_signal(barrier, inc=1, device_id=beside, device_id_type=MESH)

    def greet(step, carry):
        pl.semaphore_signal(barrier, inc=1, device_id={"mom": me ^ step}, device_id_type=MESH)
        return carry

    lax.fori_loop(1, momenta, greet, 0)
    load_vertex = pltpu.make_async_copy(vertex_ref.at[0], vertex_own, local_sem.at[0])
    load_left = pltpu.make_async_copy(left_ref.at[0], left_own, local_sem.at[1])
    load_vertex.start()
    load_left.start()
    pl.semaphore_wait(barrier, momenta + 1)

    left_moves = []
    for n in range(chunks):
        move = pltpu.make_async_remote_copy(
            src_ref=left_ref.at[0, n * rows:(n + 1) * rows],
            dst_ref=left_got.at[n * rows:(n + 1) * rows],
            send_sem=left_send.at[n], recv_sem=left_recv.at[n],
            device_id=across, device_id_type=MESH,
        )
        move.start()
        left_moves.append(move)
    vertex_move = pltpu.make_async_remote_copy(
        src_ref=vertex_ref.at[0], dst_ref=vertex_got,
        send_sem=vertex_send, recv_sem=vertex_recv,
        device_id=beside, device_id_type=MESH,
    )
    vertex_move.start()

    for j in range(per_device):
        wanted = jnp.transpose(jnp.broadcast_to(map_ref[j:j + 1, :], (8, momenta)))[:, 0:1]
        place = lax.broadcasted_iota(jnp.int32, (momenta, half), 1)
        hit = place == wanted * per_device + j
        choose[j * momenta:(j + 1) * momenta, :] = jnp.where(hit, 1.0, 0.0).astype(BF16)

    load_vertex.wait()
    flipped[row] = jnp.transpose(vertex_own[...])
    load_left.wait()
    own_scale = bubble_ref[0:1, pl.ds(pl.multiple_of(col * half, LANES), half)]
    weighted[col] = (left_own[...].astype(F32) * own_scale).astype(BF16)
    vertex_move.wait()
    flipped[1 - row] = jnp.transpose(vertex_got[...])

    first[...] = nt(flipped[col], weighted[col])

    other_scale = bubble_ref[0:1, pl.ds(pl.multiple_of((1 - col) * half, LANES), half)]
    first_moves = []
    for n in range(chunks):
        left_moves[n].wait_recv()
        here = slice(n * rows, (n + 1) * rows)
        weighted[1 - col, here, :] = (left_got[here, :].astype(F32) * other_scale).astype(BF16)
        total = first[:, here] + nt(flipped[1 - col], weighted[1 - col, here, :])
        first[:, here] = total
        first_round[row, :, here] = total.astype(BF16)
        move = pltpu.make_async_remote_copy(
            src_ref=first_round.at[row, :, here], dst_ref=first_round.at[row, :, here],
            send_sem=first_send.at[n], recv_sem=first_recv.at[n],
            device_id=beside, device_id_type=MESH,
        )
        move.start()
        first_moves.append(move)
    for move in first_moves:
        move.wait_recv()

    sent_rows = sent.reshape(sent.shape[0], half, LANES)
    got_rows = got.reshape(got.shape[0], half, LANES)
    for part in range(parts):
        here = slice(part * span, (part + 1) * span)
        total = (
            nt(first_round[0], weighted[0, here, :])
            + nt(first_round[1], weighted[1, here, :])
            + first[:, here]
            + flipped[row, :, here].astype(F32)
        ).astype(BF16)
        for b in range(blocks):
            sent_rows[part * blocks + b] = total[:, b * LANES:(b + 1) * LANES]
        these = slice(part * blocks, (part + 1) * blocks)
        pltpu.make_async_copy(sent.at[these, me], got.at[these, me], keep_sem.at[part]).start()

        def send(step, carry, these=these, part=part):
            to = me ^ step
            pltpu.make_async_remote_copy(
                src_ref=sent.at[these, to], dst_ref=got.at[these, me],
                send_sem=move_send.at[part], recv_sem=move_recv.at[part],
                device_id={"mom": to}, device_id_type=MESH,
            ).start()
            return carry

        lax.fori_loop(1, momenta, send, 0)

    out_moves = []
    for part in range(parts):
        these = slice(part * blocks, (part + 1) * blocks)
        pltpu.make_async_copy(sent.at[these, me], got.at[these, me], keep_sem.at[part]).wait()
        everyone = pl.ds(0, momenta - 1)
        pltpu.make_async_remote_copy(
            src_ref=sent.at[these, everyone], dst_ref=got.at[these, everyone],
            send_sem=move_send.at[part], recv_sem=move_recv.at[part],
            device_id={"mom": me ^ 1}, device_id_type=MESH,
        ).wait()
        values = jnp.concatenate([got_rows[part * blocks + b] for b in range(blocks)], axis=1)
        picked = jnp.dot(choose[...], values, preferred_element_type=F32)
        result[part] = picked.astype(BF16)
        for j in range(per_device):
            move = pltpu.make_async_copy(
                result.at[part, j * momenta:(j + 1) * momenta, :],
                out_ref.at[j, :, part * span:(part + 1) * span],
                out_sem.at[part, j],
            )
            move.start()
            out_moves.append(move)
    for move in left_moves + first_moves:
        move.wait_send()
    for move in out_moves:
        move.wait()


def on_device(left_part, vertex, bubble, cross_map):
    momenta = lax.axis_size("mom")
    half = vertex.shape[2]
    per_device = half // momenta
    chunks = 6 if half % (6 * LANES) == 0 else half // LANES
    parts = 3 if half % (3 * LANES) == 0 else 1
    span = half // parts
    any_space = pl.BlockSpec(memory_space=pl.ANY)
    in_vmem = pl.BlockSpec(memory_space=pltpu.VMEM)
    dma = pltpu.SemaphoreType.DMA
    square = pltpu.VMEM((half, half), BF16)
    pair = pltpu.VMEM((2, half, half), BF16)
    moved = pltpu.VMEM((half // LANES, momenta, per_device // 2, 2, LANES), BF16)
    return pl.pallas_call(
        functools.partial(kernel, momenta),
        out_shape=jax.ShapeDtypeStruct((per_device, momenta, half), BF16),
        in_specs=[any_space, any_space, in_vmem, in_vmem],
        out_specs=any_space,
        scratch_shapes=[
            square, square, square, square, pair, pair,
            pltpu.VMEM((half, half), F32), pair,
            square, moved, moved, pltpu.VMEM((parts, half, span), BF16),
            dma((2,)), dma((chunks,)), dma((chunks,)), dma, dma, dma((chunks,)), dma((chunks,)),
            dma((parts,)), dma((parts,)), dma((parts,)), dma((parts, per_device)),
        ],
        compiler_params=pltpu.CompilerParams(
            collective_id=0, has_side_effects=True, vmem_limit_bytes=56 * 2**20
        ),
        cost_estimate=pl.CostEstimate(
            flops=10 * half**3, bytes_accessed=6 * half * half, transcendentals=0
        ),
    )(left_part, vertex, bubble, cross_map)


def solution(mesh):
    in_specs = (
        P("mom", "row", "col"),
        P("mom", "row", "col"),
        P("mom", None),
        P(("col", "mom"), None),
    )
    out_specs = P(("col", "mom"), None, "row")
    return jax.shard_map(
        on_device, mesh=mesh, in_specs=in_specs, out_specs=out_specs, check_vma=False
    )
```

```python
import functools

import jax
import jax.numpy as jnp
from jax import lax
from jax.experimental import pallas as pl
from jax.experimental.pallas import tpu as pltpu
from jax.sharding import PartitionSpec as P

MESH = pl.DeviceIdType.MESH
F32 = jnp.float32
BF16 = jnp.bfloat16
LANES = 128
UNROLL = 4


def nt(lhs, rhs):
    return lax.dot_general(lhs, rhs, (((1,), (1,)), ((), ())), preferred_element_type=F32)


def kernel(
    momenta, left_ref, vertex_ref, bubble_ref, map_ref, out_ref,
    left_own, left_got, vertex_own, vertex_got, weighted, flipped, first, first_round,
    choose, sent, got,
    local_sem, left_send, left_recv, vertex_send, vertex_recv, first_send, first_recv,
    move_send, move_recv, keep_sem, round_sem,
):
    half = left_own.shape[0]
    per_device = half // momenta
    parts = move_send.shape[0]
    span = half // parts
    blocks = span // LANES
    pieces, chunks = left_send.shape[0], first_send.shape[0]
    me = lax.axis_index("mom")
    row = lax.axis_index("row")
    col = lax.axis_index("col")
    across = {"col": 1 - col}
    beside = {"row": 1 - row}

    barrier = pltpu.get_barrier_semaphore()
    rounds = round_sem.shape[0]
    pl.semaphore_signal(barrier, inc=1, device_id=across, device_id_type=MESH)
    pl.semaphore_signal(barrier, inc=1, device_id=beside, device_id_type=MESH)
    for r in range(rounds):
        pl.semaphore_signal(barrier, inc=1, device_id={"mom": me ^ (1 << r)}, device_id_type=MESH)
    load_vertex = pltpu.make_async_copy(vertex_ref.at[0], vertex_own, local_sem.at[0])
    load_left = pltpu.make_async_copy(left_ref.at[0], left_own, local_sem.at[1])
    load_vertex.start()
    load_left.start()
    pl.semaphore_wait(barrier, rounds + 2)

    left_moves = []
    for n in range(pieces):
        rows = half // pieces
        move = pltpu.make_async_remote_copy(
            src_ref=left_ref.at[0, n * rows:(n + 1) * rows],
            dst_ref=left_got.at[n * rows:(n + 1) * rows],
            send_sem=left_send.at[n], recv_sem=left_recv.at[n],
            device_id=across, device_id_type=MESH,
        )
        move.start()
        left_moves.append(move)
    vertex_move = pltpu.make_async_remote_copy(
        src_ref=vertex_ref.at[0], dst_ref=vertex_got,
        send_sem=vertex_send, recv_sem=vertex_recv,
        device_id=beside, device_id_type=MESH,
    )
    vertex_move.start()

    def call(r):
        if r < rounds:
            pl.semaphore_signal(
                round_sem.at[r], inc=1, device_id={"mom": me ^ (1 << r)}, device_id_type=MESH
            )

    def hear(r):
        if r < rounds:
            pl.semaphore_wait(round_sem.at[r], 1)
            call(r + 1)

    call(0)
    load_vertex.wait()
    flipped[row] = jnp.transpose(vertex_own[...])
    hear(0)
    load_left.wait()
    own_scale = bubble_ref[0:1, pl.ds(pl.multiple_of(col * half, LANES), half)]
    weighted[col] = (left_own[...].astype(F32) * own_scale).astype(BF16)
    hear(1)
    vertex_move.wait()
    flipped[1 - row] = jnp.transpose(vertex_got[...])
    hear(2)
    first[...] = nt(flipped[col], weighted[col])
    hear(3)
    for j in range(per_device):
        wanted = jnp.transpose(jnp.broadcast_to(map_ref[j:j + 1, :], (8, momenta)))[:, 0:1]
        place = lax.broadcasted_iota(jnp.int32, (momenta, half), 1)
        hit = place == wanted * per_device + j
        choose[j * momenta:(j + 1) * momenta, :] = jnp.where(hit, 1.0, 0.0).astype(BF16)
        if j % 2 == 1 or j == per_device - 1:
            hear(4 + j // 2)
    for r in range(4 + (per_device + 1) // 2, rounds):
        hear(r)

    other_scale = bubble_ref[0:1, pl.ds(pl.multiple_of((1 - col) * half, LANES), half)]
    first_moves = []
    rows = half // chunks
    each = pieces // chunks
    for n in range(chunks):
        for move in left_moves[n * each:(n + 1) * each]:
            move.wait_recv()
        here = slice(n * rows, (n + 1) * rows)
        weighted[1 - col, here, :] = (left_got[here, :].astype(F32) * other_scale).astype(BF16)
        total = first[:, here] + nt(flipped[1 - col], weighted[1 - col, here, :])
        first[:, here] = total
        first_round[row, :, here] = total.astype(BF16)
        move = pltpu.make_async_remote_copy(
            src_ref=first_round.at[row, :, here], dst_ref=first_round.at[row, :, here],
            send_sem=first_send.at[n], recv_sem=first_recv.at[n],
            device_id=beside, device_id_type=MESH,
        )
        move.start()
        first_moves.append(move)
    for part in range(parts):
        here = slice(part * span, (part + 1) * span)
        first[:, here] = (
            first[:, here]
            + flipped[row, :, here].astype(F32)
            + nt(first_round[row], weighted[row, here, :])
        )
    for move in first_moves:
        move.wait_recv()

    sent_rows = sent.reshape(sent.shape[0], half, LANES)
    got_rows = got.reshape(got.shape[0], half, LANES)
    for part in range(parts):
        here = slice(part * span, (part + 1) * span)
        total = (
            first[:, here] + nt(first_round[1 - row], weighted[1 - row, here, :])
        ).astype(BF16)
        for b in range(blocks):
            sent_rows[part * blocks + b] = total[:, b * LANES:(b + 1) * LANES]
        these = slice(part * blocks, (part + 1) * blocks)
        pltpu.make_async_copy(sent.at[these, me], got.at[these, me], keep_sem.at[part]).start()

        def send(step, carry, these=these, part=part):
            to = me ^ step
            pltpu.make_async_remote_copy(
                src_ref=sent.at[these, to], dst_ref=got.at[these, me],
                send_sem=move_send.at[part], recv_sem=move_recv.at[part],
                device_id={"mom": to}, device_id_type=MESH,
            ).start()
            return carry

        lax.fori_loop(1, momenta, send, 0, unroll=UNROLL)

    for part in range(parts):
        these = slice(part * blocks, (part + 1) * blocks)
        pltpu.make_async_copy(sent.at[these, me], got.at[these, me], keep_sem.at[part]).wait()
        everyone = pl.ds(0, momenta - 1)
        pltpu.make_async_remote_copy(
            src_ref=sent.at[these, everyone], dst_ref=got.at[these, everyone],
            send_sem=move_send.at[part], recv_sem=move_recv.at[part],
            device_id={"mom": me ^ 1}, device_id_type=MESH,
        ).wait()
        values = jnp.concatenate([got_rows[part * blocks + b] for b in range(blocks)], axis=1)
        picked = jnp.dot(choose[...], values, preferred_element_type=F32)
        for j in range(per_device):
            out_ref[j, :, part * span:(part + 1) * span] = (
                picked[j * momenta:(j + 1) * momenta].astype(BF16)
            )
    for move in left_moves + first_moves:
        move.wait_send()


def on_device(left_part, vertex, bubble, cross_map):
    momenta = lax.axis_size("mom")
    half = vertex.shape[2]
    per_device = half // momenta
    chunks = half // LANES
    pieces = 2 * chunks
    parts = 3 if half % (3 * LANES) == 0 else 1
    span = half // parts
    any_space = pl.BlockSpec(memory_space=pl.ANY)
    in_vmem = pl.BlockSpec(memory_space=pltpu.VMEM)
    dma = pltpu.SemaphoreType.DMA
    square = pltpu.VMEM((half, half), BF16)
    pair = pltpu.VMEM((2, half, half), BF16)
    moved = pltpu.VMEM((half // LANES, momenta, per_device // 2, 2, LANES), BF16)
    return pl.pallas_call(
        functools.partial(kernel, momenta),
        out_shape=pltpu.VMEM((per_device, momenta, half), BF16),
        in_specs=[any_space, any_space, in_vmem, in_vmem],
        out_specs=in_vmem,
        scratch_shapes=[
            square, square, square, square, pair, pair,
            pltpu.VMEM((half, half), F32), pair,
            square, moved, moved,
            dma((2,)), dma((pieces,)), dma((pieces,)), dma, dma, dma((chunks,)), dma((chunks,)),
            dma((parts,)), dma((parts,)), dma((parts,)),
            pltpu.SemaphoreType.REGULAR((momenta.bit_length() - 1,)),
        ],
        compiler_params=pltpu.CompilerParams(
            collective_id=0, has_side_effects=True, vmem_limit_bytes=56 * 2**20
        ),
        cost_estimate=pl.CostEstimate(
            flops=10 * half**3, bytes_accessed=6 * half * half, transcendentals=0
        ),
    )(left_part, vertex, bubble, cross_map)


def solution(mesh):
    in_specs = (
        P("mom", "row", "col"),
        P("mom", "row", "col"),
        P("mom", None),
        P(("col", "mom"), None),
    )
    out_specs = P(("col", "mom"), None, "row")
    return jax.shard_map(
        on_device, mesh=mesh, in_specs=in_specs, out_specs=out_specs, check_vma=False
    )
```

```python
import functools

import jax
import jax.numpy as jnp
from jax import lax
from jax.experimental import pallas as pl
from jax.experimental.pallas import tpu as pltpu
from jax.sharding import PartitionSpec as P

MESH = pl.DeviceIdType.MESH
F32 = jnp.float32
BF16 = jnp.bfloat16
LANES = 128
UNROLL = 4


def nt(lhs, rhs):
    return lax.dot_general(lhs, rhs, (((1,), (1,)), ((), ())), preferred_element_type=F32)


def kernel(
    momenta, left_ref, vertex_ref, bubble_ref, map_ref, out_ref,
    left_own, left_got, vertex_own, vertex_got, weighted, flipped, first, first_round,
    choose, sent, got,
    local_sem, left_send, left_recv, vertex_send, vertex_recv, first_send, first_recv,
    move_send, move_recv, keep_sem, round_sem,
):
    half = left_own.shape[0]
    per_device = half // momenta
    parts = move_send.shape[0]
    span = half // parts
    blocks = span // LANES
    pieces, chunks = left_send.shape[0], first_send.shape[0]
    me = lax.axis_index("mom")
    row = lax.axis_index("row")
    col = lax.axis_index("col")
    across = {"col": 1 - col}
    beside = {"row": 1 - row}

    barrier = pltpu.get_barrier_semaphore()
    rounds = round_sem.shape[0]
    pl.semaphore_signal(barrier, inc=1, device_id=across, device_id_type=MESH)
    pl.semaphore_signal(barrier, inc=1, device_id=beside, device_id_type=MESH)
    for r in range(rounds):
        pl.semaphore_signal(barrier, inc=1, device_id={"mom": me ^ (1 << r)}, device_id_type=MESH)
    load_vertex = pltpu.make_async_copy(vertex_ref.at[0], vertex_own, local_sem.at[0])
    load_left = pltpu.make_async_copy(left_ref.at[0], left_own, local_sem.at[1])
    load_vertex.start()
    load_left.start()
    pl.semaphore_wait(barrier, rounds + 2)

    left_moves = []
    for n in range(pieces):
        rows = half // pieces
        move = pltpu.make_async_remote_copy(
            src_ref=left_ref.at[0, n * rows:(n + 1) * rows],
            dst_ref=left_got.at[n * rows:(n + 1) * rows],
            send_sem=left_send.at[n], recv_sem=left_recv.at[n],
            device_id=across, device_id_type=MESH,
        )
        move.start()
        left_moves.append(move)
    vertex_move = pltpu.make_async_remote_copy(
        src_ref=vertex_ref.at[0], dst_ref=vertex_got,
        send_sem=vertex_send, recv_sem=vertex_recv,
        device_id=beside, device_id_type=MESH,
    )
    vertex_move.start()

    def call(r):
        if r < rounds:
            pl.semaphore_signal(
                round_sem.at[r], inc=1, device_id={"mom": me ^ (1 << r)}, device_id_type=MESH
            )

    def hear(r):
        if r < rounds:
            pl.semaphore_wait(round_sem.at[r], 1)
            call(r + 1)

    call(0)
    load_vertex.wait()
    flipped[row] = jnp.transpose(vertex_own[...])
    hear(0)
    load_left.wait()
    own_scale = bubble_ref[0:1, pl.ds(pl.multiple_of(col * half, LANES), half)]
    weighted[col] = (left_own[...].astype(F32) * own_scale).astype(BF16)
    hear(1)
    vertex_move.wait()
    flipped[1 - row] = jnp.transpose(vertex_got[...])
    hear(2)
    first[...] = nt(flipped[col], weighted[col])
    hear(3)
    for j in range(per_device):
        wanted = jnp.transpose(jnp.broadcast_to(map_ref[j:j + 1, :], (8, momenta)))[:, 0:1]
        place = lax.broadcasted_iota(jnp.int32, (momenta, half), 1)
        hit = place == wanted * per_device + j
        choose[j * momenta:(j + 1) * momenta, :] = jnp.where(hit, 1.0, 0.0).astype(BF16)
        if j % 2 == 1 or j == per_device - 1:
            hear(4 + j // 2)
    for r in range(4 + (per_device + 1) // 2, rounds):
        hear(r)

    other_scale = bubble_ref[0:1, pl.ds(pl.multiple_of((1 - col) * half, LANES), half)]
    first_moves = []
    rows = half // chunks
    each = pieces // chunks
    for n in range(chunks):
        for move in left_moves[n * each:(n + 1) * each]:
            move.wait_recv()
        here = slice(n * rows, (n + 1) * rows)
        weighted[1 - col, here, :] = (left_got[here, :].astype(F32) * other_scale).astype(BF16)
        total = first[:, here] + nt(flipped[1 - col], weighted[1 - col, here, :])
        first[:, here] = total
        first_round[row, :, here] = total.astype(BF16)
        move = pltpu.make_async_remote_copy(
            src_ref=first_round.at[row, :, here], dst_ref=first_round.at[row, :, here],
            send_sem=first_send.at[n], recv_sem=first_recv.at[n],
            device_id=beside, device_id_type=MESH,
        )
        move.start()
        first_moves.append(move)
    for part in range(parts):
        here = slice(part * span, (part + 1) * span)
        first[:, here] = (
            first[:, here]
            + flipped[row, :, here].astype(F32)
            + nt(first_round[row], weighted[row, here, :])
        )
    for move in first_moves:
        move.wait_recv()

    sent_rows = sent.reshape(sent.shape[0], half, LANES)
    got_rows = got.reshape(got.shape[0], half, LANES)
    for part in range(parts):
        here = slice(part * span, (part + 1) * span)
        total = (
            first[:, here] + nt(first_round[1 - row], weighted[1 - row, here, :])
        ).astype(BF16)
        for b in range(blocks):
            sent_rows[part * blocks + b] = total[:, b * LANES:(b + 1) * LANES]
        these = slice(part * blocks, (part + 1) * blocks)
        pltpu.make_async_copy(sent.at[these, me], got.at[these, me], keep_sem.at[part]).start()

        def send(step, carry, these=these, part=part):
            to = me ^ step
            pltpu.make_async_remote_copy(
                src_ref=sent.at[these, to], dst_ref=got.at[these, me],
                send_sem=move_send.at[part], recv_sem=move_recv.at[part],
                device_id={"mom": to}, device_id_type=MESH,
            ).start()
            return carry

        lax.fori_loop(1, momenta, send, 0, unroll=UNROLL)

    for part in range(parts):
        these = slice(part * blocks, (part + 1) * blocks)
        pltpu.make_async_copy(sent.at[these, me], got.at[these, me], keep_sem.at[part]).wait()
        everyone = pl.ds(0, momenta - 1)
        pltpu.make_async_remote_copy(
            src_ref=sent.at[these, everyone], dst_ref=got.at[these, everyone],
            send_sem=move_send.at[part], recv_sem=move_recv.at[part],
            device_id={"mom": me ^ 1}, device_id_type=MESH,
        ).wait()
        values = jnp.concatenate([got_rows[part * blocks + b] for b in range(blocks)], axis=1)
        picked = jnp.dot(choose[...], values, preferred_element_type=F32)
        for j in range(per_device):
            out_ref[j, :, part * span:(part + 1) * span] = (
                picked[j * momenta:(j + 1) * momenta].astype(BF16)
            )
    for move in left_moves + first_moves:
        move.wait_send()


def on_device(left_part, vertex, bubble, cross_map):
    momenta = lax.axis_size("mom")
    half = vertex.shape[2]
    per_device = half // momenta
    chunks = half // LANES
    pieces = 2 * chunks
    parts = 6 if half % (6 * LANES) == 0 else 1
    span = half // parts
    any_space = pl.BlockSpec(memory_space=pl.ANY)
    in_vmem = pl.BlockSpec(memory_space=pltpu.VMEM)
    dma = pltpu.SemaphoreType.DMA
    square = pltpu.VMEM((half, half), BF16)
    pair = pltpu.VMEM((2, half, half), BF16)
    moved = pltpu.VMEM((half // LANES, momenta, per_device // 2, 2, LANES), BF16)
    return pl.pallas_call(
        functools.partial(kernel, momenta),
        out_shape=pltpu.VMEM((per_device, momenta, half), BF16),
        in_specs=[any_space, any_space, in_vmem, in_vmem],
        out_specs=in_vmem,
        scratch_shapes=[
            square, square, square, square, pair, pair,
            pltpu.VMEM((half, half), F32), pair,
            square, moved, moved,
            dma((2,)), dma((pieces,)), dma((pieces,)), dma, dma, dma((chunks,)), dma((chunks,)),
            dma((parts,)), dma((parts,)), dma((parts,)),
            pltpu.SemaphoreType.REGULAR((momenta.bit_length() - 1,)),
        ],
        compiler_params=pltpu.CompilerParams(
            collective_id=0, has_side_effects=True, vmem_limit_bytes=56 * 2**20
        ),
        cost_estimate=pl.CostEstimate(
            flops=10 * half**3, bytes_accessed=6 * half * half, transcendentals=0
        ),
    )(left_part, vertex, bubble, cross_map)


def solution(mesh):
    in_specs = (
        P("mom", "row", "col"),
        P("mom", "row", "col"),
        P("mom", None),
        P(("col", "mom"), None),
    )
    out_specs = P(("col", "mom"), None, "row")
    return jax.shard_map(
        on_device, mesh=mesh, in_specs=in_specs, out_specs=out_specs, check_vma=False
    )
```
